512 devices in a mesh: pool: 32 (over z, x), tp: 16 (over y, core).
Axes of the slice: x: 4, y: 8, z: 8, core: 2. Of those that a mesh axis runs over, the one named last changes fastest.
Arguments:
- pool_kv: bfloat16 [2048, 2, 1024, 128], P('pool', None, 'tp'), may hold values from -6 to 6
- queries: bfloat16 [64, 128, 8192], P('pool', None, 'tp'), may hold values from -9 to 9
- new_kv: bfloat16 [64, 2, 1024, 128], P('pool', None, 'tp'), may hold values from -9 to 9
- page_table: int32 [64, 32], replicated, may hold values from -1 to 2047, as said below
- prefix_pages: int32 [64], replicated, may hold values from 8 to 32, as said below
Outputs:
- attended: bfloat16 [64, 128, 8192], P('pool', None, 'tp')
- landed: bfloat16 [64, 2, 1024, 128], P('pool', None, 'tp')
The draws below stay inside these ranges and needn't reach their ends.
Inputs may be any that keep to these rules, and one draw needn't show every extreme that they name: `page_table`: entry j < prefix_pages[r] of row r is owner * 64 + slot, the owner being the pool index that holds the page; later entries are -1. The pages of one request lie on distinct owners, so an owner holds at most one page of each request; no slot holds two pages. `prefix_pages`: some request has a prefix of 32 pages.
All inputs are finite; a program needn't handle non-finite values.
Results may differ from the reference program's by a relative error of at most 0.0052.
Values may be sent and summed in bfloat16 or wider, within the bound.
No kernel may reach another device: no remote copies, remote signals or barrier semaphores. Data moves between devices by JAX's collectives and lax.ppermute only.
A program may use at most 64 MiB of HBM per device.

```python
import math
import jax
import jax.numpy as jnp
from jax import lax

HD = 128
KVH = 8
QH = 64
PAGE = 128
SUF = 128
REQUESTS = 64
SLOTS = 64
MAXP = 32
N_POOL = 32


def page_lengths(key):
    key = jax.random.fold_in(key, 11)
    key_one, key_two = jax.random.split(key)
    lengths = jax.random.randint(key_one, (REQUESTS,), MAXP // 4, MAXP + 1)
    longest = jax.random.randint(key_two, (), 0, REQUESTS)
    return jnp.where(jnp.arange(REQUESTS) == longest, MAXP, lengths).astype(jnp.int32)


def draw_prefix_pages(key, part):
    return page_lengths(key)


def draw_page_table(key, part):
    lengths = page_lengths(key)
    key = jax.random.fold_in(key, 5)
    key_one, key_two = jax.random.split(key)
    owners = jax.vmap(lambda subkey: jax.random.permutation(subkey, N_POOL))(jax.random.split(key_one, REQUESTS))
    places = jax.vmap(lambda subkey: jax.random.permutation(subkey, REQUESTS))(jax.random.split(key_two, N_POOL))
    request_ids = jnp.arange(REQUESTS)[:, None]
    slot_ids = places[owners, request_ids]
    slot_table = owners * SLOTS + slot_ids
    page_spots = jnp.arange(MAXP)[None, :]
    return jnp.where(page_spots < lengths[:, None], slot_table[:, :MAXP], -1).astype(jnp.int32)


def draw_queries(key, part):
    key = jax.random.fold_in(key, 3)
    key_one = jax.random.fold_in(key, 0)
    samples = jax.random.truncated_normal(key_one, -6.0, 6.0, (REQUESTS, SUF, KVH, QH // KVH, HD))
    return samples.reshape(REQUESTS, SUF, QH * HD).astype(jnp.bfloat16)


def draw_new_kv(key, part):
    key = jax.random.fold_in(key, 7)
    key_one, key_two = jax.random.split(key)
    key_part = jax.random.truncated_normal(key_one, -6.0, 6.0, (REQUESTS, SUF, KVH, HD))
    value_part = jax.random.truncated_normal(key_two, -6.0, 6.0, (REQUESTS, SUF, KVH, HD))
    key_part = jnp.transpose(key_part, (0, 2, 3, 1)).reshape(REQUESTS, KVH * HD, SUF)
    value_part = jnp.transpose(value_part, (0, 2, 3, 1)).reshape(REQUESTS, KVH * HD, SUF)
    return jnp.stack([key_part, value_part], axis=1).astype(jnp.bfloat16)


def steps_of(key, dims, pieces, low, high):
    factor_of, own = 1.0, jax.random.fold_in(key, 6)
    for axis_at, blocks in pieces:
        heights = jnp.exp(jax.random.uniform(jax.random.fold_in(own, axis_at), (blocks,), jnp.float32, low / len(pieces), high / len(pieces)))
        factor_of = factor_of * jnp.repeat(heights, dims[axis_at] // blocks).reshape([-1 if axis == axis_at else 1 for axis in range(len(dims))])
    return factor_of


def bell_draw(own_key, dims, scale, reach, cuts=(), kind=jnp.bfloat16):
    values = scale * jax.random.normal(own_key, dims, jnp.float32)
    if cuts:
        values = values * steps_of(own_key, dims, cuts, -0.22, 0.18)
    return jnp.clip(values, -reach, reach).astype(kind)


def setup_inputs(seed: int = 0) -> dict:
    streams_of = jax.random.split(jax.random.key(seed), 6)
    return {
        "pool_kv": bell_draw(streams_of[0], (N_POOL * SLOTS, 2, KVH * HD, PAGE), 1.0, 6.0, ((0, 32), (2, 16))),
        "queries": draw_queries(jax.random.fold_in(streams_of[5], 71), 0),
        "new_kv": draw_new_kv(jax.random.fold_in(streams_of[5], 71), 0),
        "page_table": draw_page_table(jax.random.fold_in(streams_of[5], 71), 0),
        "prefix_pages": draw_prefix_pages(jax.random.fold_in(streams_of[5], 71), 0),
    }


def rope_tables(positions, head_width):
    indices = jnp.arange(head_width // 2, dtype=jnp.float32)
    inverse = jnp.power(jnp.float32(1000000.0), -2.0 * indices / head_width)
    angles = positions.astype(jnp.float32)[:, None] * inverse[None, :]
    angles = jnp.concatenate([angles, angles], axis=1)
    return (jnp.cos(angles), jnp.sin(angles))

def rotate(values, cosine_table, sine_table):
    half_size = values.shape[-1] // 2
    turned = jnp.concatenate([-values[..., half_size:], values[..., :half_size]], axis=-1)
    return values * cosine_table + turned * sine_table

def reference(pool_kv, queries, new_kv, page_table, prefix_pages):
    groups = QH // KVH
    score_scale = 1.0 / math.sqrt(HD)
    causal = jnp.arange(SUF)[None, :] <= jnp.arange(SUF)[:, None]

    def one_request(inputs):
        query_rows, fresh_kv, page_row, length = inputs
        positions = length * PAGE + jnp.arange(SUF, dtype=jnp.int32)
        cosine_table, sine_table = rope_tables(positions, HD)
        query_heads = query_rows.reshape(SUF, KVH, groups, HD).astype(jnp.float32)
        rotated_q = rotate(query_heads, cosine_table[:, None, None, :], sine_table[:, None, None, :]).astype(jnp.bfloat16)
        rotated_q = lax.optimization_barrier(rotated_q)
        fresh_keys = jnp.transpose(fresh_kv[0].reshape(KVH, HD, SUF), (2, 0, 1)).astype(jnp.float32)
        rotated_k = rotate(fresh_keys, cosine_table[:, None, :], sine_table[:, None, :]).astype(jnp.bfloat16)
        rotated_k = lax.optimization_barrier(rotated_k)
        fresh_values = jnp.transpose(fresh_kv[1].reshape(KVH, HD, SUF), (2, 0, 1))
        fetched = pool_kv[jnp.maximum(page_row, 0)]
        page_keys = jnp.transpose(fetched[:, 0].reshape(MAXP, KVH, HD, PAGE), (0, 3, 1, 2)).reshape(MAXP * PAGE, KVH, HD)
        page_values = jnp.transpose(fetched[:, 1].reshape(MAXP, KVH, HD, PAGE), (0, 3, 1, 2)).reshape(MAXP * PAGE, KVH, HD)
        all_keys = jnp.concatenate([page_keys, rotated_k], axis=0).astype(jnp.float32)
        all_values = jnp.concatenate([page_values, fresh_values], axis=0).astype(jnp.float32)
        live_keys = jnp.repeat(jnp.arange(MAXP) < length, PAGE)
        allowed = jnp.concatenate([jnp.broadcast_to(live_keys[None, :], (SUF, MAXP * PAGE)), causal], axis=1)
        scores = jnp.einsum('skgd,lkd->kgsl', rotated_q.astype(jnp.float32), all_keys) * score_scale
        scores = jnp.where(allowed[None, None], scores, -jnp.inf)
        largest = lax.optimization_barrier(jnp.max(scores, axis=-1, keepdims=True))
        weights = jnp.exp(scores - largest)
        totals = lax.optimization_barrier(jnp.sum(weights, axis=-1))
        rounded = lax.optimization_barrier(weights.astype(jnp.bfloat16))
        summed = jnp.einsum('kgsl,lkd->skgd', rounded.astype(jnp.float32), all_values)
        attended = summed / jnp.transpose(totals, (2, 0, 1))[..., None]
        written_keys = jnp.transpose(rotated_k, (1, 2, 0)).reshape(KVH * HD, SUF)
        return (attended.reshape(SUF, QH * HD).astype(jnp.bfloat16), written_keys)
    attended, written_keys = lax.map(one_request, (queries, new_kv, page_table, prefix_pages))
    landed = jnp.stack([written_keys, new_kv[:, 1]], axis=1)
    return (attended, jnp.roll(landed, REQUESTS // 2, axis=0))
```

```python
import functools
import math

import jax
import jax.numpy as jnp
from jax import lax
from jax.experimental import pallas as pl
from jax.experimental.pallas import tpu as pltpu
from jax.sharding import Mesh
from jax.sharding import PartitionSpec as P

MIB = 1024 * 1024
GROUP = ("pool", "core")


def swap_cores(array):
    return lax.ppermute(array, "core", [(0, 1), (1, 0)])


def from_behind(array, axis, by):
    devices = lax.axis_size(axis)
    return lax.ppermute(array, axis, [(i, (i + by) % devices) for i in range(devices)])


def angles_of(positions, head_width):
    indices = jnp.arange(head_width // 2, dtype=jnp.float32)
    inverse = jnp.power(jnp.float32(1000000.0), -2.0 * indices / head_width)
    return positions.astype(jnp.float32)[:, None] * inverse[None, :]


def pack_kernel(part, slots_ref, pool_ref, out_ref, sem):
    count = out_ref.shape[0]

    @pl.loop(0, count, unroll=8)
    def _(r):
        pltpu.make_async_copy(pool_ref.at[slots_ref[r], part], out_ref.at[r], sem).start()

    pltpu.make_async_copy(out_ref, out_ref, sem).wait()


def pack(part, slots, pool_kv):
    count = slots.shape[0]
    _, _, half, page = pool_kv.shape
    return pl.pallas_call(
        functools.partial(pack_kernel, part),
        grid_spec=pltpu.PrefetchScalarGridSpec(
            num_scalar_prefetch=1,
            grid=(1,),
            in_specs=[pl.BlockSpec(memory_space=pl.ANY)],
            out_specs=pl.BlockSpec(memory_space=pl.ANY),
            scratch_shapes=[pltpu.SemaphoreType.DMA],
        ),
        out_shape=jax.ShapeDtypeStruct((count, half, page), pool_kv.dtype),
        compiler_params=pltpu.CompilerParams(vmem_limit_bytes=2 * MIB),
        cost_estimate=pl.CostEstimate(
            flops=0, bytes_accessed=2 * count * half * page * 2, transcendentals=0
        ),
        name="pack_pages",
    )(slots, pool_kv)


def weigh_kernel(heads, live_ref, q_ref, cos_ref, sin_ref, keys_ref, fresh_ref,
                 w_ref, wf_ref, totals_ref, rq_ref, scores_ref, own_ref, peak_ref):
    tokens = q_ref.shape[1]
    width = cos_ref.shape[1]
    pairs = w_ref.shape[1]
    page = fresh_ref.shape[1]
    rows = heads * tokens
    scale = 1.0 / math.sqrt(width)
    for h in range(heads):
        x = q_ref[0, :, h * width:(h + 1) * width].astype(jnp.float32)
        turned = pltpu.roll(x, width // 2, 1)
        rq_ref[h * tokens:(h + 1) * tokens, :] = (
            x * cos_ref[...] + turned * sin_ref[...]
        ).astype(jnp.bfloat16)
    rq = rq_ref[...]
    own = jnp.dot(rq, fresh_ref[...], preferred_element_type=jnp.float32) * scale
    token = lax.rem(lax.broadcasted_iota(jnp.int32, (rows, page), 0), tokens)
    key = lax.broadcasted_iota(jnp.int32, (rows, page), 1)
    own = jnp.where(key <= token, own, -jnp.inf)
    own_ref[...] = own
    peak_ref[...] = own
    lane = lax.broadcasted_iota(jnp.int32, (1, 2 * page), 1)

    @pl.loop(0, pairs)
    def _(g):
        block = jnp.concatenate([keys_ref[2 * g], keys_ref[2 * g + 1]], axis=1)
        one = jnp.where(live_ref[2 * g] > 0, 0.0, -1e30)
        two = jnp.where(live_ref[2 * g + 1] > 0, 0.0, -1e30)
        bias = jnp.where(lane < page, one, two)
        s = jnp.dot(rq, block, preferred_element_type=jnp.float32) * scale + bias
        scores_ref[g] = s
        peak_ref[...] = jnp.maximum(
            peak_ref[...], jnp.maximum(s[:, :page], s[:, page:])
        )

    largest = jnp.max(peak_ref[...], axis=1, keepdims=True)
    w = jnp.exp(own_ref[...] - largest)
    wf_ref[0] = w.astype(jnp.bfloat16)
    own_ref[...] = w
    peak_ref[...] = jnp.broadcast_to(largest, (rows, page))

    @pl.loop(0, pairs)
    def _(g):
        top = peak_ref[...]
        a = jnp.exp(scores_ref[g, :, :page] - top)
        b = jnp.exp(scores_ref[g, :, page:] - top)
        w_ref[0, g, :, :page] = a.astype(jnp.bfloat16)
        w_ref[0, g, :, page:] = b.astype(jnp.bfloat16)
        own_ref[...] += a + b

    totals_ref[0] = jnp.broadcast_to(
        jnp.sum(own_ref[...], axis=1, keepdims=True), (rows, page)
    )


def weigh(live, q, cosine, sine, keys, fresh):
    sets, tokens, wide = q.shape
    pages, width, page = keys.shape
    heads = wide // width
    rows = heads * tokens
    pairs = pages // 2
    whole = lambda *shape: pl.BlockSpec(shape, lambda s, *_: (0,) * len(shape))
    each = lambda *shape: pl.BlockSpec((1,) + shape, lambda s, *_: (s,) + (0,) * len(shape))
    return pl.pallas_call(
        functools.partial(weigh_kernel, heads),
        grid_spec=pltpu.PrefetchScalarGridSpec(
            num_scalar_prefetch=1,
            grid=(sets,),
            in_specs=[
                each(tokens, wide),
                whole(tokens, width),
                whole(tokens, width),
                whole(pages, width, page),
                whole(width, page),
            ],
            out_specs=[
                each(pairs, rows, 2 * page),
                each(rows, page),
                each(rows, page),
            ],
            scratch_shapes=[
                pltpu.VMEM((rows, width), jnp.bfloat16),
                pltpu.VMEM((pairs, rows, 2 * page), jnp.float32),
                pltpu.VMEM((rows, page), jnp.float32),
                pltpu.VMEM((rows, page), jnp.float32),
            ],
        ),
        out_shape=[
            jax.ShapeDtypeStruct((sets, pairs, rows, 2 * page), jnp.bfloat16),
            jax.ShapeDtypeStruct((sets, rows, page), jnp.bfloat16),
            jax.ShapeDtypeStruct((sets, rows, page), jnp.float32),
        ],
        compiler_params=pltpu.CompilerParams(vmem_limit_bytes=32 * MIB),
        cost_estimate=pl.CostEstimate(
            flops=2 * sets * rows * pages * page * width,
            bytes_accessed=sets * rows * pages * page * 2,
            transcendentals=sets * rows * pages * page,
        ),
        name="weigh_keys",
    )(live, q, cosine, sine, keys, fresh)


def gather_kernel(heads, w_ref, wf_ref, totals_ref, values_ref, fresh_ref, out_ref, acc_ref):
    step = pl.program_id(0)
    tokens, wide = out_ref.shape
    width = wide // heads
    contract_last = (((1,), (1,)), ((), ()))

    @pl.when(step == 0)
    def _():
        acc_ref[...] = lax.dot_general(
            wf_ref[0], fresh_ref[...], contract_last, preferred_element_type=jnp.float32
        )

    total = acc_ref[...]
    for g in range(w_ref.shape[1]):
        block = jnp.concatenate([values_ref[2 * g], values_ref[2 * g + 1]], axis=1)
        total += lax.dot_general(
            w_ref[0, g], block, contract_last, preferred_element_type=jnp.float32
        )
    acc_ref[...] = total

    @pl.when(step == pl.num_programs(0) - 1)
    def _():
        done = (acc_ref[...] / totals_ref[0]).astype(jnp.bfloat16)
        for h in range(heads):
            out_ref[:, h * width:(h + 1) * width] = done[h * tokens:(h + 1) * tokens, :]


def attend(which, tokens, w, wf, totals, values, fresh):
    _, pairs, rows, two_pages = w.shape
    page = two_pages // 2
    width = fresh.shape[0]
    heads = rows // tokens
    steps = 4
    per = pairs // steps
    return pl.pallas_call(
        functools.partial(gather_kernel, heads),
        grid=(steps,),
        in_specs=[
            pl.BlockSpec((1, per, rows, two_pages), lambda s: (which, s, 0, 0)),
            pl.BlockSpec((1, rows, page), lambda s: (which, 0, 0)),
            pl.BlockSpec((1, rows, page), lambda s: (which, 0, 0)),
            pl.BlockSpec((2 * per, width, page), lambda s: (s, 0, 0)),
            pl.BlockSpec((width, page), lambda s: (0, 0)),
        ],
        out_specs=pl.BlockSpec((tokens, heads * width), lambda s: (0, 0)),
        scratch_shapes=[pltpu.VMEM((rows, width), jnp.float32)],
        out_shape=jax.ShapeDtypeStruct((tokens, heads * width), jnp.bfloat16),
        compiler_params=pltpu.CompilerParams(vmem_limit_bytes=12 * MIB),
        cost_estimate=pl.CostEstimate(
            flops=2 * rows * pairs * two_pages * width,
            bytes_accessed=rows * pairs * two_pages * 2,
            transcendentals=0,
        ),
        name="attend_values",
    )(w, wf, totals, values, fresh)


def on_device(pool_kv, queries, new_kv, page_table, prefix_pages):
    pool_count = lax.axis_size("pool")
    pool_rank = lax.axis_index("pool")
    core = lax.axis_index("core")
    lower_half = core == 0
    slot_count, _, half_width, page_len = pool_kv.shape
    head_width = 2 * half_width
    local_requests, suffix_len, _ = queries.shape
    owner_of = page_table // slot_count
    slot_of = jnp.sum(jnp.where(owner_of == pool_rank, page_table % slot_count, 0), axis=1)

    sent_keys = pack(0, slot_of, pool_kv)
    page_keys = lax.all_to_all(sent_keys, GROUP, split_axis=0, concat_axis=0, tiled=True)
    sent_values = pack(1, slot_of, pool_kv)
    page_values = lax.all_to_all(sent_values, GROUP, split_axis=0, concat_axis=0, tiled=True)
    page_keys = page_keys.reshape(pool_count, head_width, page_len)
    page_values = page_values.reshape(pool_count, head_width, page_len)

    first_row = pool_rank * local_requests
    own_owners = lax.dynamic_index_in_dim(owner_of, first_row + core, 0, keepdims=False)
    owner_ids = jnp.arange(pool_count, dtype=jnp.int32)
    live = jnp.any(own_owners[None, :] == owner_ids[:, None], axis=1).astype(jnp.int32)
    own_lengths = lax.dynamic_slice_in_dim(prefix_pages, first_row, local_requests, 0)

    given = lax.dynamic_index_in_dim(queries, 1 - core, 0, keepdims=False)
    kept = lax.dynamic_index_in_dim(queries, core, 0, keepdims=False)
    other_fresh = swap_cores(new_kv)
    taken = swap_cores(given)

    positions = own_lengths[:, None] * page_len + jnp.arange(suffix_len, dtype=jnp.int32)
    angles = angles_of(positions.reshape(-1), head_width).reshape(
        local_requests, suffix_len, half_width
    )
    cosine, sine = jnp.cos(angles), jnp.sin(angles)
    own_cosine = lax.dynamic_index_in_dim(cosine, core, 0, keepdims=False)
    own_sine = lax.dynamic_index_in_dim(sine, core, 0, keepdims=False)
    q_cosine = jnp.concatenate([own_cosine, own_cosine], axis=1)
    q_sine = jnp.concatenate([-own_sine, own_sine], axis=1)

    first = jnp.where(lower_half, new_kv[:, 0], other_fresh[:, 0]).astype(jnp.float32)
    second = jnp.where(lower_half, other_fresh[:, 0], new_kv[:, 0]).astype(jnp.float32)
    k_cosine = jnp.swapaxes(cosine, 1, 2)
    k_sine = jnp.swapaxes(sine, 1, 2)
    rotated_first = (first * k_cosine - second * k_sine).astype(jnp.bfloat16)
    rotated_second = (second * k_cosine + first * k_sine).astype(jnp.bfloat16)
    own_keys = jnp.where(lower_half, rotated_first, rotated_second)
    landing = jnp.stack([own_keys, new_kv[:, 1]], axis=1)
    landed = from_behind(landing, "pool", pool_count // 2)

    fresh_keys = lax.dynamic_index_in_dim(
        jnp.concatenate([rotated_first, rotated_second], axis=1), core, 0, keepdims=False
    )
    mine = lax.dynamic_index_in_dim(new_kv[:, 1], core, 0, keepdims=False)
    theirs = lax.dynamic_index_in_dim(other_fresh[:, 1], core, 0, keepdims=False)
    fresh_values = jnp.where(
        lower_half,
        jnp.concatenate([mine, theirs], axis=0),
        jnp.concatenate([theirs, mine], axis=0),
    )

    w, wf, totals = weigh(
        live, jnp.stack([taken, kept], axis=0), q_cosine, q_sine, page_keys, fresh_keys
    )
    for_partner = attend(0, suffix_len, w, wf, totals, page_values, fresh_values)
    from_partner = swap_cores(for_partner)
    stays = attend(1, suffix_len, w, wf, totals, page_values, fresh_values)
    attended = jnp.where(
        lower_half,
        jnp.stack([stays, from_partner], axis=0),
        jnp.stack([from_partner, stays], axis=0),
    )
    return (attended, landed)


def solution(mesh):
    pool_count, tp_count = mesh.devices.shape
    cores = Mesh(mesh.devices.reshape(pool_count, tp_count // 2, 2), ("pool", "head", "core"))
    tp = ("head", "core")
    return jax.shard_map(
        on_device,
        mesh=cores,
        in_specs=(
            P("pool", None, tp, None),
            P("pool", None, tp),
            P("pool", None, tp, None),
            P(),
            P(),
        ),
        out_specs=(P("pool", None, tp), P("pool", None, tp, None)),
        check_vma=False,
    )
```

```python
import functools
import math

import jax
import jax.numpy as jnp
from jax import lax
from jax.experimental import pallas as pl
from jax.experimental.pallas import tpu as pltpu
from jax.sharding import Mesh
from jax.sharding import PartitionSpec as P

MIB = 1024 * 1024
GROUP = ("pool", "core")
CONTRACT_LAST = (((1,), (1,)), ((), ()))
GROUPED = 4
STEPS = 4


def factor_of(width):
    return math.log2(math.e) / math.sqrt(width)


def swap_cores(array):
    return lax.ppermute(array, "core", [(0, 1), (1, 0)])


def from_behind(array, axis, by):
    devices = lax.axis_size(axis)
    return lax.ppermute(array, axis, [(i, (i + by) % devices) for i in range(devices)])


def angles_of(positions, head_width):
    indices = jnp.arange(head_width // 2, dtype=jnp.float32)
    inverse = jnp.power(jnp.float32(1000000.0), -2.0 * indices / head_width)
    return positions.astype(jnp.float32)[:, None] * inverse[None, :]


def pack_kernel(slots_ref, pool_ref, out_ref, sem):
    count = out_ref.shape[0]

    @pl.loop(0, count, unroll=8)
    def _(r):
        pltpu.make_async_copy(pool_ref.at[slots_ref[r]], out_ref.at[r], sem).start()

    pltpu.make_async_copy(out_ref, out_ref, sem).wait()


def pack(slots, pool_kv):
    shape = (slots.shape[0],) + pool_kv.shape[1:]
    return pl.pallas_call(
        pack_kernel,
        grid_spec=pltpu.PrefetchScalarGridSpec(
            num_scalar_prefetch=1,
            grid=(1,),
            in_specs=[pl.BlockSpec(memory_space=pl.ANY)],
            out_specs=pl.BlockSpec(memory_space=pl.ANY),
            scratch_shapes=[pltpu.SemaphoreType.DMA],
        ),
        out_shape=jax.ShapeDtypeStruct(shape, pool_kv.dtype),
        compiler_params=pltpu.CompilerParams(vmem_limit_bytes=2 * MIB),
        cost_estimate=pl.CostEstimate(
            flops=0, bytes_accessed=4 * math.prod(shape), transcendentals=0
        ),
        name="pack_pages",
    )(slots, pool_kv)


def own_scores(rq, fresh_keys, tokens):
    rows, page = rq.shape[0], fresh_keys.shape[1]
    own = jnp.dot(rq, fresh_keys, preferred_element_type=jnp.float32)
    token = lax.rem(lax.broadcasted_iota(jnp.int32, (rows, page), 0), tokens)
    key = lax.broadcasted_iota(jnp.int32, (rows, page), 1)
    return jnp.where(key <= token, own, -1e30)


def prepare_kernel(heads, factor, q_ref, cos_ref, sin_ref, keys_ref, values_ref,
                   rq_ref, state_ref):
    tokens = q_ref.shape[1]
    width = cos_ref.shape[1]
    rows = heads * tokens
    parts = []
    for h in range(heads):
        x = q_ref[0, :, h * width:(h + 1) * width].astype(jnp.float32)
        turned = pltpu.roll(x, width // 2, 1)
        parts.append((x * cos_ref[...] + turned * sin_ref[...]).astype(jnp.bfloat16))
    rq = jnp.concatenate(parts, axis=0)
    own = own_scores(rq, keys_ref[...], tokens)
    shift = jnp.max(own, axis=1, keepdims=True).astype(jnp.bfloat16).astype(jnp.float32)
    lane = lax.broadcasted_iota(jnp.int32, (rows, width), 1)
    extra = jnp.where(lane == 0, -shift, jnp.where(lane == 1, 1.0, 0.0))
    rq_ref[0, :, :width] = rq
    rq_ref[0, :, width:] = extra.astype(jnp.bfloat16)
    w = jnp.exp2((own - shift) * factor)
    state_ref[0, :, :width] = lax.dot_general(
        w.astype(jnp.bfloat16), values_ref[...], CONTRACT_LAST,
        preferred_element_type=jnp.float32,
    )
    state_ref[0, :, width:] = jnp.broadcast_to(jnp.sum(w, axis=1, keepdims=True), (rows, width))


def prepare(q, cosine, sine, fresh_keys, fresh_values):
    sets, tokens, wide = q.shape
    width, page = fresh_keys.shape
    heads = wide // width
    rows = heads * tokens
    whole = lambda *shape: pl.BlockSpec(shape, lambda s: (0,) * len(shape))
    each = lambda *shape: pl.BlockSpec((1,) + shape, lambda s: (s,) + (0,) * len(shape))
    return pl.pallas_call(
        functools.partial(prepare_kernel, heads, factor_of(width)),
        grid=(sets,),
        in_specs=[
            each(tokens, wide),
            whole(tokens, width),
            whole(tokens, width),
            whole(width, page),
            whole(width, page),
        ],
        out_specs=[each(rows, 2 * width), each(rows, 2 * width)],
        out_shape=[
            jax.ShapeDtypeStruct((sets, rows, 2 * width), jnp.bfloat16),
            jax.ShapeDtypeStruct((sets, rows, 2 * width), jnp.float32),
        ],
        compiler_params=pltpu.CompilerParams(vmem_limit_bytes=16 * MIB),
        cost_estimate=pl.CostEstimate(
            flops=4 * sets * rows * page * width,
            bytes_accessed=sets * rows * 2 * width * 6,
            transcendentals=sets * rows * page,
        ),
        name="prepare_queries",
    )(q, cosine, sine, fresh_keys, fresh_values)


def attend_kernel(heads, factor, live_ref, rq_ref, state_ref, kv_ref, keys_ref, values_ref,
                  all_ref, out_ref, acc_ref, page_ref, top_ref, sem):
    step = pl.program_id(0)
    tokens, wide = out_ref.shape
    width = wide // heads
    rows = heads * tokens
    page = kv_ref.shape[4]
    count = kv_ref.shape[0]
    first = step * count

    @pl.when(step == 0)
    def _():
        acc_ref[...] = state_ref[0]

    row = lax.broadcasted_iota(jnp.int32, (width, page), 0)

    def flags(p):
        hidden = jnp.where(live_ref[p] > 0, 0.0, -1e30)
        return jnp.where(row == 0, 1.0, jnp.where(row == 1, hidden, 0.0)).astype(jnp.bfloat16)

    ones = jnp.ones((width, GROUPED * page), jnp.bfloat16)
    rq = rq_ref[0]
    for at in range(0, count, GROUPED):
        weights, values = [], []
        for p in range(at, at + GROUPED, 2):
            keys = jnp.concatenate(
                [
                    jnp.concatenate(
                        [kv_ref[p + i, 0, 0], kv_ref[p + i, 1, 0], flags(first + p + i)], axis=0
                    )
                    for i in range(2)
                ],
                axis=1,
            )
            s = jnp.dot(rq, keys, preferred_element_type=jnp.float32)
            weights.append(jnp.exp2(s * factor).astype(jnp.bfloat16))
        for p in range(at, at + GROUPED):
            values.append(jnp.concatenate([kv_ref[p, 0, 1], kv_ref[p, 1, 1]], axis=0))
        block = jnp.concatenate([jnp.concatenate(values, axis=1), ones], axis=0)
        acc_ref[...] += lax.dot_general(
            jnp.concatenate(weights, axis=1), block, CONTRACT_LAST,
            preferred_element_type=jnp.float32,
        )

    @pl.when(step == pl.num_programs(0) - 1)
    def _():
        largest_total = jnp.max(acc_ref[:, width:])

        @pl.when(jnp.logical_not(largest_total <= 1e30))
        def _():
            exact(factor, tokens, width, live_ref, rq_ref, keys_ref, values_ref, all_ref,
                  acc_ref, page_ref, top_ref, sem)

        done = (acc_ref[:, :width] / acc_ref[:, width:]).astype(jnp.bfloat16)
        for h in range(heads):
            out_ref[:, h * width:(h + 1) * width] = done[h * tokens:(h + 1) * tokens, :]


def exact(factor, tokens, width, live_ref, rq_ref, keys_ref, values_ref, all_ref,
          acc_ref, page_ref, top_ref, sem):
    rows = rq_ref.shape[1]
    pages = all_ref.shape[0]
    half = width // 2
    rq = rq_ref[0, :, :width]
    own = own_scores(rq, keys_ref[...], tokens)
    top_ref[...] = own

    def scores_of(p):
        copy = pltpu.make_async_copy(all_ref.at[p], page_ref, sem)
        copy.start()
        copy.wait()
        keys = jnp.concatenate([page_ref[0, 0], page_ref[1, 0]], axis=0)
        hidden = jnp.where(live_ref[p] > 0, 0.0, -1e30)
        return jnp.dot(rq, keys, preferred_element_type=jnp.float32) + hidden

    @pl.loop(0, pages)
    def _(p):
        top_ref[...] = jnp.maximum(top_ref[...], scores_of(p))

    top_ref[...] = jnp.broadcast_to(
        jnp.max(top_ref[...], axis=1, keepdims=True), top_ref.shape
    )
    w = jnp.exp2((own - top_ref[...]) * factor)
    acc_ref[:, :width] = lax.dot_general(
        w.astype(jnp.bfloat16), values_ref[...], CONTRACT_LAST,
        preferred_element_type=jnp.float32,
    )
    acc_ref[:, width:] = jnp.broadcast_to(jnp.sum(w, axis=1, keepdims=True), (rows, width))

    @pl.loop(0, pages)
    def _(p):
        w = jnp.exp2((scores_of(p) - top_ref[...]) * factor)
        values = jnp.concatenate([page_ref[0, 1], page_ref[1, 1]], axis=0)
        acc_ref[:, :width] += lax.dot_general(
            w.astype(jnp.bfloat16), values, CONTRACT_LAST, preferred_element_type=jnp.float32
        )
        acc_ref[:, width:] += jnp.broadcast_to(
            jnp.sum(w, axis=1, keepdims=True), (rows, width)
        )


def attend(which, tokens, live, rq, state, arrived, fresh_keys, fresh_values):
    _, rows, double = rq.shape
    pages, _, _, half, page = arrived.shape
    width = double // 2
    heads = rows // tokens
    steps = STEPS
    per = pages // steps
    return pl.pallas_call(
        functools.partial(attend_kernel, heads, factor_of(width)),
        grid_spec=pltpu.PrefetchScalarGridSpec(
            num_scalar_prefetch=1,
            grid=(steps,),
            in_specs=[
                pl.BlockSpec((1, rows, double), lambda s, *_: (which, 0, 0)),
                pl.BlockSpec((1, rows, double), lambda s, *_: (which, 0, 0)),
                pl.BlockSpec((per, 2, 2, half, page), lambda s, *_: (s, 0, 0, 0, 0)),
                pl.BlockSpec((width, page), lambda s, *_: (0, 0)),
                pl.BlockSpec((width, page), lambda s, *_: (0, 0)),
                pl.BlockSpec(memory_space=pl.ANY),
            ],
            out_specs=pl.BlockSpec((tokens, heads * width), lambda s, *_: (0, 0)),
            scratch_shapes=[
                pltpu.VMEM((rows, double), jnp.float32),
                pltpu.VMEM((2, 2, half, page), jnp.bfloat16),
                pltpu.VMEM((rows, page), jnp.float32),
                pltpu.SemaphoreType.DMA,
            ],
        ),
        out_shape=jax.ShapeDtypeStruct((tokens, heads * width), jnp.bfloat16),
        compiler_params=pltpu.CompilerParams(vmem_limit_bytes=40 * MIB),
        cost_estimate=pl.CostEstimate(
            flops=4 * rows * pages * page * width,
            bytes_accessed=pages * width * page * 4,
            transcendentals=rows * pages * page,
        ),
        name="attend_pages",
    )(live, rq, state, arrived, fresh_keys, fresh_values, arrived)


def on_device(pool_kv, queries, new_kv, page_table, prefix_pages):
    pool_count = lax.axis_size("pool")
    pool_rank = lax.axis_index("pool")
    core = lax.axis_index("core")
    lower_half = core == 0
    slot_count, _, half_width, page_len = pool_kv.shape
    head_width = 2 * half_width
    local_requests, suffix_len, _ = queries.shape
    owner_of = page_table // slot_count
    slot_of = jnp.sum(jnp.where(owner_of == pool_rank, page_table % slot_count, 0), axis=1)

    arrived = lax.all_to_all(
        pack(slot_of, pool_kv), GROUP, split_axis=0, concat_axis=0, tiled=True
    ).reshape(pool_count, 2, 2, half_width, page_len)

    first_row = pool_rank * local_requests
    own_owners = lax.dynamic_index_in_dim(owner_of, first_row + core, 0, keepdims=False)
    owner_ids = jnp.arange(pool_count, dtype=jnp.int32)
    live = jnp.any(own_owners[None, :] == owner_ids[:, None], axis=1).astype(jnp.int32)
    own_lengths = lax.dynamic_slice_in_dim(prefix_pages, first_row, local_requests, 0)

    given = lax.dynamic_index_in_dim(queries, 1 - core, 0, keepdims=False)
    kept = lax.dynamic_index_in_dim(queries, core, 0, keepdims=False)
    other_fresh = swap_cores(new_kv)
    taken = swap_cores(given)

    positions = own_lengths[:, None] * page_len + jnp.arange(suffix_len, dtype=jnp.int32)
    angles = angles_of(positions.reshape(-1), head_width).reshape(
        local_requests, suffix_len, half_width
    )
    cosine, sine = jnp.cos(angles), jnp.sin(angles)
    own_cosine = lax.dynamic_index_in_dim(cosine, core, 0, keepdims=False)
    own_sine = lax.dynamic_index_in_dim(sine, core, 0, keepdims=False)
    q_cosine = jnp.concatenate([own_cosine, own_cosine], axis=1)
    q_sine = jnp.concatenate([-own_sine, own_sine], axis=1)

    first = jnp.where(lower_half, new_kv[:, 0], other_fresh[:, 0]).astype(jnp.float32)
    second = jnp.where(lower_half, other_fresh[:, 0], new_kv[:, 0]).astype(jnp.float32)
    k_cosine = jnp.swapaxes(cosine, 1, 2)
    k_sine = jnp.swapaxes(sine, 1, 2)
    rotated_first = (first * k_cosine - second * k_sine).astype(jnp.bfloat16)
    rotated_second = (second * k_cosine + first * k_sine).astype(jnp.bfloat16)
    own_keys = jnp.where(lower_half, rotated_first, rotated_second)
    landing = jnp.stack([own_keys, new_kv[:, 1]], axis=1)
    landed = from_behind(landing, "pool", pool_count // 2)

    fresh_keys = lax.dynamic_index_in_dim(
        jnp.concatenate([rotated_first, rotated_second], axis=1), core, 0, keepdims=False
    )
    mine = lax.dynamic_index_in_dim(new_kv[:, 1], core, 0, keepdims=False)
    theirs = lax.dynamic_index_in_dim(other_fresh[:, 1], core, 0, keepdims=False)
    fresh_values = jnp.where(
        lower_half,
        jnp.concatenate([mine, theirs], axis=0),
        jnp.concatenate([theirs, mine], axis=0),
    )

    rq, state = prepare(
        jnp.stack([taken, kept], axis=0), q_cosine, q_sine, fresh_keys, fresh_values
    )
    arrived, landed = lax.optimization_barrier((arrived, landed))
    inputs = (live, rq, state, arrived, fresh_keys, fresh_values)
    for_partner = attend(0, suffix_len, *inputs)
    from_partner = swap_cores(for_partner)
    stays = attend(1, suffix_len, *inputs)
    attended = jnp.where(
        lower_half,
        jnp.stack([stays, from_partner], axis=0),
        jnp.stack([from_partner, stays], axis=0),
    )
    return (attended, landed)


def solution(mesh):
    pool_count, tp_count = mesh.devices.shape
    cores = Mesh(mesh.devices.reshape(pool_count, tp_count // 2, 2), ("pool", "head", "core"))
    tp = ("head", "core")
    return jax.shard_map(
        on_device,
        mesh=cores,
        in_specs=(
            P("pool", None, tp, None),
            P("pool", None, tp),
            P("pool", None, tp, None),
            P(),
            P(),
        ),
        out_specs=(P("pool", None, tp), P("pool", None, tp, None)),
        check_vma=False,
    )
```

```python
import functools
import math

import jax
import jax.numpy as jnp
from jax import lax
from jax.experimental import pallas as pl
from jax.experimental.pallas import tpu as pltpu
from jax.sharding import Mesh
from jax.sharding import PartitionSpec as P

MIB = 1024 * 1024
GROUP = ("pool", "core")
CONTRACT_LAST = (((1,), (1,)), ((), ()))
GROUPED = 8
UNROLL = 4


def factor_of(width):
    return math.log2(math.e) / math.sqrt(width)


def swap_cores(array):
    return lax.ppermute(array, "core", [(0, 1), (1, 0)])


def from_behind(array, axis, by):
    devices = lax.axis_size(axis)
    return lax.ppermute(array, axis, [(i, (i + by) % devices) for i in range(devices)])


def angles_of(positions, head_width):
    indices = jnp.arange(head_width // 2, dtype=jnp.float32)
    inverse = jnp.power(jnp.float32(1000000.0), -2.0 * indices / head_width)
    return positions.astype(jnp.float32)[:, None] * inverse[None, :]


def pack_kernel(table_ref, pool_ref, out_ref, slots_ref, scalars_ref, sem):
    count = out_ref.shape[0]
    slot_count = pool_ref.shape[0]
    slot = table_ref[...] - lax.axis_index("pool") * slot_count
    mine = jnp.logical_and(slot >= 0, slot < slot_count)
    slots_ref[...] = jnp.sum(jnp.where(mine, slot, 0), axis=0, keepdims=True)
    copy = pltpu.make_async_copy(slots_ref, scalars_ref, sem.at[0])
    copy.start()
    copy.wait()

    @pl.loop(0, count, unroll=8)
    def _(r):
        pltpu.make_async_copy(
            pool_ref.at[scalars_ref[0, r]], out_ref.at[r], sem.at[1]
        ).start()

    pltpu.make_async_copy(out_ref, out_ref, sem.at[1]).wait()


def pack(page_table, pool_kv):
    requests, most = page_table.shape
    shape = (requests,) + pool_kv.shape[1:]
    return pl.pallas_call(
        pack_kernel,
        in_specs=[
            pl.BlockSpec(memory_space=pltpu.VMEM),
            pl.BlockSpec(memory_space=pltpu.HBM),
        ],
        out_specs=pl.BlockSpec(memory_space=pltpu.HBM),
        scratch_shapes=[
            pltpu.VMEM((1, requests), jnp.int32),
            pltpu.SMEM((1, requests), jnp.int32),
            pltpu.SemaphoreType.DMA((2,)),
        ],
        out_shape=jax.ShapeDtypeStruct(shape, pool_kv.dtype),
        compiler_params=pltpu.CompilerParams(vmem_limit_bytes=2 * MIB),
        cost_estimate=pl.CostEstimate(
            flops=0, bytes_accessed=4 * math.prod(shape), transcendentals=0
        ),
        name="pack_pages",
    )(page_table.T, pool_kv)


def own_scores(rq, fresh_keys, tokens):
    rows, page = rq.shape[0], fresh_keys.shape[1]
    own = jnp.dot(rq, fresh_keys, preferred_element_type=jnp.float32)
    token = lax.rem(lax.broadcasted_iota(jnp.int32, (rows, page), 0), tokens)
    key = lax.broadcasted_iota(jnp.int32, (rows, page), 1)
    return jnp.where(key <= token, own, -1e30)


def prepare_kernel(heads, factor, q_ref, cos_ref, sin_ref, keys_ref, values_ref,
                   rq_ref, state_ref):
    tokens = q_ref.shape[1]
    width = cos_ref.shape[1]
    rows = heads * tokens
    parts = []
    for h in range(heads):
        x = q_ref[0, :, h * width:(h + 1) * width].astype(jnp.float32)
        turned = pltpu.roll(x, width // 2, 1)
        parts.append((x * cos_ref[...] + turned * sin_ref[...]).astype(jnp.bfloat16))
    rq = jnp.concatenate(parts, axis=0)
    own = own_scores(rq, keys_ref[...], tokens)
    shift = jnp.max(own, axis=1, keepdims=True).astype(jnp.bfloat16).astype(jnp.float32)
    lane = lax.broadcasted_iota(jnp.int32, (rows, width), 1)
    extra = jnp.where(lane == 0, -shift, jnp.where(lane == 1, 1.0, 0.0))
    rq_ref[0, :, :width] = rq
    rq_ref[0, :, width:] = extra.astype(jnp.bfloat16)
    w = jnp.exp2((own - shift) * factor)
    state_ref[0, :, :width] = lax.dot_general(
        w.astype(jnp.bfloat16), values_ref[...], CONTRACT_LAST,
        preferred_element_type=jnp.float32,
    )
    state_ref[0, :, width:] = jnp.broadcast_to(jnp.sum(w, axis=1, keepdims=True), (rows, width))


def prepare(q, cosine, sine, fresh_keys, fresh_values):
    sets, tokens, wide = q.shape
    width, page = fresh_keys.shape
    heads = wide // width
    rows = heads * tokens
    whole = lambda *shape: pl.BlockSpec(shape, lambda s: (0,) * len(shape))
    each = lambda *shape: pl.BlockSpec((1,) + shape, lambda s: (s,) + (0,) * len(shape))
    return pl.pallas_call(
        functools.partial(prepare_kernel, heads, factor_of(width)),
        grid=(sets,),
        in_specs=[
            each(tokens, wide),
            whole(tokens, width),
            whole(tokens, width),
            whole(width, page),
            whole(width, page),
        ],
        out_specs=[each(rows, 2 * width), each(rows, 2 * width)],
        out_shape=[
            jax.ShapeDtypeStruct((sets, rows, 2 * width), jnp.bfloat16),
            jax.ShapeDtypeStruct((sets, rows, 2 * width), jnp.float32),
        ],
        compiler_params=pltpu.CompilerParams(vmem_limit_bytes=16 * MIB),
        cost_estimate=pl.CostEstimate(
            flops=4 * sets * rows * page * width,
            bytes_accessed=sets * rows * 2 * width * 6,
            transcendentals=sets * rows * page,
        ),
        name="prepare_queries",
    )(q, cosine, sine, fresh_keys, fresh_values)


def attend_kernel(heads, factor, landing, live_ref, rq_ref, state_ref, all_ref, keys_ref,
                  values_ref, *refs):
    if landing:
        landed_ref, whole_ref, placed_ref, acc_ref, top_ref, out_ref, sem = refs
        place = pltpu.make_async_copy(landed_ref, placed_ref, sem.at[0])
        place.start()
    else:
        out_ref, acc_ref, top_ref = refs
    tokens, wide = out_ref.shape
    width = wide // heads
    page = all_ref.shape[4]
    pages = all_ref.shape[0]
    row = lax.broadcasted_iota(jnp.int32, (width, page), 0)

    def flags(p):
        hidden = jnp.where(live_ref[p] > 0, 0.0, -1e30)
        return jnp.where(row == 0, 1.0, jnp.where(row == 1, hidden, 0.0)).astype(jnp.bfloat16)

    def part_of(p, which):
        return jnp.concatenate([all_ref[p, 0, which], all_ref[p, 1, which]], axis=0)

    ones = jnp.ones((width, GROUPED * page), jnp.bfloat16)
    acc_ref[...] = state_ref[int(landing)]
    rq = rq_ref[int(landing)]

    @pl.loop(0, pages // GROUPED, unroll=UNROLL)
    def _(g):
        at = g * GROUPED
        weights = []
        for i in range(0, GROUPED, 2):
            keys = jnp.concatenate(
                [
                    jnp.concatenate([part_of(at + i + j, 0), flags(at + i + j)], axis=0)
                    for j in range(2)
                ],
                axis=1,
            )
            s = jnp.dot(rq, keys, preferred_element_type=jnp.float32)
            weights.append(jnp.exp2(s * factor).astype(jnp.bfloat16))
        values = jnp.concatenate([part_of(at + i, 1) for i in range(GROUPED)], axis=1)
        acc_ref[...] += lax.dot_general(
            jnp.concatenate(weights, axis=1), jnp.concatenate([values, ones], axis=0),
            CONTRACT_LAST, preferred_element_type=jnp.float32,
        )

    @pl.when(jnp.logical_not(jnp.max(acc_ref[:, width:]) <= 1e30))
    def _():
        exact(factor, tokens, width, live_ref, rq_ref.at[int(landing)], keys_ref, values_ref,
              all_ref, acc_ref, top_ref)

    done = (acc_ref[:, :width] / acc_ref[:, width:]).astype(jnp.bfloat16)
    for h in range(heads):
        out_ref[:, h * width:(h + 1) * width] = done[h * tokens:(h + 1) * tokens, :]
    if landing:
        keep = pltpu.make_async_copy(out_ref, whole_ref.at[lax.axis_index("core")], sem.at[1])
        keep.start()
        keep.wait()
        place.wait()


def exact(factor, tokens, width, live_ref, rq_ref, keys_ref, values_ref, all_ref, acc_ref, top_ref):
    rows = rq_ref.shape[0]
    pages = all_ref.shape[0]
    rq = rq_ref[:, :width]
    own = own_scores(rq, keys_ref[...], tokens)
    top_ref[...] = own

    def part_of(p, which):
        return jnp.concatenate([all_ref[p, 0, which], all_ref[p, 1, which]], axis=0)

    def scores_of(p):
        hidden = jnp.where(live_ref[p] > 0, 0.0, -1e30)
        return jnp.dot(rq, part_of(p, 0), preferred_element_type=jnp.float32) + hidden

    @pl.loop(0, pages)
    def _(p):
        top_ref[...] = jnp.maximum(top_ref[...], scores_of(p))

    top_ref[...] = jnp.broadcast_to(
        jnp.max(top_ref[...], axis=1, keepdims=True), top_ref.shape
    )
    w = jnp.exp2((own - top_ref[...]) * factor)
    acc_ref[:, :width] = lax.dot_general(
        w.astype(jnp.bfloat16), values_ref[...], CONTRACT_LAST,
        preferred_element_type=jnp.float32,
    )
    acc_ref[:, width:] = jnp.broadcast_to(jnp.sum(w, axis=1, keepdims=True), (rows, width))

    @pl.loop(0, pages)
    def _(p):
        w = jnp.exp2((scores_of(p) - top_ref[...]) * factor)
        acc_ref[:, :width] += lax.dot_general(
            w.astype(jnp.bfloat16), part_of(p, 1), CONTRACT_LAST, preferred_element_type=jnp.float32
        )
        acc_ref[:, width:] += jnp.broadcast_to(
            jnp.sum(w, axis=1, keepdims=True), (rows, width)
        )


def attend(tokens, live, rq, state, arrived, fresh_keys, fresh_values, landed=None):
    _, rows, double = rq.shape
    pages, _, _, half, page = arrived.shape
    width = double // 2
    heads = rows // tokens
    shape = (tokens, heads * width)
    landing = landed is not None
    vmem = pl.BlockSpec(memory_space=pltpu.VMEM)
    hbm = pl.BlockSpec(memory_space=pltpu.HBM)
    scratch = [pltpu.VMEM((rows, double), jnp.float32), pltpu.VMEM((rows, page), jnp.float32)]
    if landing:
        more, more_specs = [landed], [vmem]
        out_shape = [
            jax.ShapeDtypeStruct((2,) + shape, jnp.bfloat16),
            jax.ShapeDtypeStruct(landed.shape, landed.dtype),
        ]
        out_specs = [hbm, hbm]
        scratch += [pltpu.VMEM(shape, jnp.bfloat16), pltpu.SemaphoreType.DMA((2,))]
    else:
        more, more_specs = [], []
        out_shape, out_specs = jax.ShapeDtypeStruct(shape, jnp.bfloat16), vmem
    return pl.pallas_call(
        functools.partial(attend_kernel, heads, factor_of(width), landing),
        in_specs=[pl.BlockSpec(memory_space=pltpu.SMEM)] + [vmem] * 5 + more_specs,
        out_specs=out_specs,
        scratch_shapes=scratch,
        out_shape=out_shape,
        compiler_params=pltpu.CompilerParams(vmem_limit_bytes=24 * MIB),
        cost_estimate=pl.CostEstimate(
            flops=4 * rows * pages * page * width,
            bytes_accessed=pages * width * page * 4,
            transcendentals=rows * pages * page,
        ),
        name="attend_kept" if landing else "attend_sent",
    )(live, rq, state, arrived, fresh_keys, fresh_values, *more)


def on_device(pool_kv, queries, new_kv, page_table, prefix_pages):
    pool_count = lax.axis_size("pool")
    pool_rank = lax.axis_index("pool")
    core = lax.axis_index("core")
    lower_half = core == 0
    slot_count, _, half_width, page_len = pool_kv.shape
    head_width = 2 * half_width
    local_requests, suffix_len, _ = queries.shape
    owner_of = page_table // slot_count
    arrived = lax.all_to_all(
        pack(page_table, pool_kv), GROUP, split_axis=0, concat_axis=0, tiled=True
    ).reshape(pool_count, 2, 2, half_width, page_len)

    first_row = pool_rank * local_requests
    own_owners = lax.dynamic_index_in_dim(owner_of, first_row + core, 0, keepdims=False)
    owner_ids = jnp.arange(pool_count, dtype=jnp.int32)
    live = jnp.any(own_owners[None, :] == owner_ids[:, None], axis=1).astype(jnp.int32)
    own_lengths = lax.dynamic_slice_in_dim(prefix_pages, first_row, local_requests, 0)

    given = lax.dynamic_index_in_dim(queries, 1 - core, 0, keepdims=False)
    kept = lax.dynamic_index_in_dim(queries, core, 0, keepdims=False)
    other_fresh = swap_cores(new_kv)
    taken = swap_cores(given)

    positions = own_lengths[:, None] * page_len + jnp.arange(suffix_len, dtype=jnp.int32)
    angles = angles_of(positions.reshape(-1), head_width).reshape(
        local_requests, suffix_len, half_width
    )
    cosine, sine = jnp.cos(angles), jnp.sin(angles)
    own_cosine = lax.dynamic_index_in_dim(cosine, core, 0, keepdims=False)
    own_sine = lax.dynamic_index_in_dim(sine, core, 0, keepdims=False)
    q_cosine = jnp.concatenate([own_cosine, own_cosine], axis=1)
    q_sine = jnp.concatenate([-own_sine, own_sine], axis=1)

    first = jnp.where(lower_half, new_kv[:, 0], other_fresh[:, 0]).astype(jnp.float32)
    second = jnp.where(lower_half, other_fresh[:, 0], new_kv[:, 0]).astype(jnp.float32)
    k_cosine = jnp.swapaxes(cosine, 1, 2)
    k_sine = jnp.swapaxes(sine, 1, 2)
    rotated_first = (first * k_cosine - second * k_sine).astype(jnp.bfloat16)
    rotated_second = (second * k_cosine + first * k_sine).astype(jnp.bfloat16)
    own_keys = jnp.where(lower_half, rotated_first, rotated_second)
    landing = jnp.stack([own_keys, new_kv[:, 1]], axis=1)
    landed = from_behind(landing, "pool", pool_count // 2)

    fresh_keys = lax.dynamic_index_in_dim(
        jnp.concatenate([rotated_first, rotated_second], axis=1), core, 0, keepdims=False
    )
    mine = lax.dynamic_index_in_dim(new_kv[:, 1], core, 0, keepdims=False)
    theirs = lax.dynamic_index_in_dim(other_fresh[:, 1], core, 0, keepdims=False)
    fresh_values = jnp.where(
        lower_half,
        jnp.concatenate([mine, theirs], axis=0),
        jnp.concatenate([theirs, mine], axis=0),
    )

    rq, state = prepare(
        jnp.stack([taken, kept], axis=0), q_cosine, q_sine, fresh_keys, fresh_values
    )
    inputs = (live, rq, state, arrived, fresh_keys, fresh_values)
    for_partner = attend(suffix_len, *inputs)
    from_partner = swap_cores(for_partner)
    attended, landed = attend(suffix_len, *inputs, landed)
    attended = lax.dynamic_update_index_in_dim(attended, from_partner, 1 - core, 0)
    return (attended, landed)


def solution(mesh):
    pool_count, tp_count = mesh.devices.shape
    cores = Mesh(mesh.devices.reshape(pool_count, tp_count // 2, 2), ("pool", "head", "core"))
    tp = ("head", "core")
    return jax.shard_map(
        on_device,
        mesh=cores,
        in_specs=(
            P("pool", None, tp, None),
            P("pool", None, tp),
            P("pool", None, tp, None),
            P(),
            P(),
        ),
        out_specs=(P("pool", None, tp), P("pool", None, tp, None)),
        check_vma=False,
    )
```

```python
import functools
import math

import jax
import jax.numpy as jnp
from jax import lax
from jax.experimental import pallas as pl
from jax.experimental.pallas import tpu as pltpu
from jax.sharding import Mesh
from jax.sharding import PartitionSpec as P

MIB = 1024 * 1024
GROUP = ("pool", "core")
CONTRACT_LAST = (((1,), (1,)), ((), ()))
GROUPED = 8


def factor_of(width):
    return math.log2(math.e) / math.sqrt(width)


def in_hbm(array):
    return pltpu.with_memory_space_constraint(array, pltpu.HBM)


def swap_cores(array):
    return lax.ppermute(array, "core", [(0, 1), (1, 0)])


def from_behind(array, axis, by):
    devices = lax.axis_size(axis)
    return lax.ppermute(array, axis, [(i, (i + by) % devices) for i in range(devices)])


def angles_of(positions, head_width):
    indices = jnp.arange(head_width // 2, dtype=jnp.float32)
    inverse = jnp.power(jnp.float32(1000000.0), -2.0 * indices / head_width)
    return positions.astype(jnp.float32)[:, None] * inverse[None, :]


def pack_kernel(table_ref, pool_ref, out_ref, held_ref, rows_ref, slots_ref, scalars_ref, sem):
    count = out_ref.shape[0]
    slot_count = pool_ref.shape[0]
    table = pltpu.make_async_copy(table_ref, rows_ref, sem.at[0])
    table.start()
    part = slot_count // 8
    for i in range(8):
        span = pl.ds(i * part, part)
        pltpu.make_async_copy(pool_ref.at[span], held_ref.at[span], sem.at[1]).start()
    table.wait()
    slot = rows_ref[...] - lax.axis_index("pool") * slot_count
    mine = jnp.logical_and(slot >= 0, slot < slot_count)
    slots_ref[...] = jnp.sum(jnp.where(mine, slot, 0), axis=0, keepdims=True)
    copy = pltpu.make_async_copy(slots_ref, scalars_ref, sem.at[2])
    copy.start()
    copy.wait()
    pltpu.make_async_copy(pool_ref, held_ref, sem.at[1]).wait()

    @pl.loop(0, count, unroll=16)
    def _(r):
        pltpu.make_async_copy(
            held_ref.at[scalars_ref[0, r]], out_ref.at[r], sem.at[3]
        ).start()

    pltpu.make_async_copy(out_ref, out_ref, sem.at[3]).wait()


def pack(page_table, pool_kv):
    requests, most = page_table.shape
    shape = (requests,) + pool_kv.shape[1:]
    hbm = pl.BlockSpec(memory_space=pltpu.HBM)
    return pl.pallas_call(
        pack_kernel,
        in_specs=[hbm, hbm],
        out_specs=hbm,
        scratch_shapes=[
            pltpu.VMEM(pool_kv.shape, pool_kv.dtype),
            pltpu.VMEM((most, requests), jnp.int32),
            pltpu.VMEM((1, requests), jnp.int32),
            pltpu.SMEM((1, requests), jnp.int32),
            pltpu.SemaphoreType.DMA((4,)),
        ],
        out_shape=jax.ShapeDtypeStruct(shape, pool_kv.dtype),
        compiler_params=pltpu.CompilerParams(vmem_limit_bytes=8 * MIB),
        cost_estimate=pl.CostEstimate(
            flops=0, bytes_accessed=4 * math.prod(shape), transcendentals=0
        ),
        name="pack_pages",
    )(in_hbm(page_table.T), in_hbm(pool_kv))


def own_scores(rq, fresh_keys, tokens):
    rows, page = rq.shape[0], fresh_keys.shape[1]
    own = jnp.dot(rq, fresh_keys, preferred_element_type=jnp.float32)
    token = lax.rem(lax.broadcasted_iota(jnp.int32, (rows, page), 0), tokens)
    key = lax.broadcasted_iota(jnp.int32, (rows, page), 1)
    return jnp.where(key <= token, own, -1e30)


def prepare_kernel(heads, factor, q_ref, cos_ref, sin_ref, keys_ref, values_ref,
                   rq_ref, state_ref):
    tokens = q_ref.shape[0]
    width = cos_ref.shape[1]
    rows = heads * tokens
    parts = []
    for h in range(heads):
        x = q_ref[:, h * width:(h + 1) * width].astype(jnp.float32)
        turned = pltpu.roll(x, width // 2, 1)
        parts.append((x * cos_ref[...] + turned * sin_ref[...]).astype(jnp.bfloat16))
    rq = jnp.concatenate(parts, axis=0)
    own = own_scores(rq, keys_ref[...], tokens)
    shift = jnp.max(own, axis=1, keepdims=True).astype(jnp.bfloat16).astype(jnp.float32)
    lane = lax.broadcasted_iota(jnp.int32, (rows, width), 1)
    extra = jnp.where(lane == 0, -shift, jnp.where(lane == 1, 1.0, 0.0))
    rq_ref[:, :width] = rq
    rq_ref[:, width:] = extra.astype(jnp.bfloat16)
    w = jnp.exp2((own - shift) * factor)
    state_ref[:, :width] = lax.dot_general(
        w.astype(jnp.bfloat16), values_ref[...], CONTRACT_LAST,
        preferred_element_type=jnp.float32,
    )
    state_ref[:, width:] = jnp.broadcast_to(jnp.sum(w, axis=1, keepdims=True), (rows, width))


def prepare(q, cosine, sine, fresh_keys, fresh_values):
    tokens, wide = q.shape
    width, page = fresh_keys.shape
    heads = wide // width
    rows = heads * tokens
    vmem = pl.BlockSpec(memory_space=pltpu.VMEM)
    return pl.pallas_call(
        functools.partial(prepare_kernel, heads, factor_of(width)),
        in_specs=[vmem] * 5,
        out_specs=[vmem] * 2,
        out_shape=[
            jax.ShapeDtypeStruct((rows, 2 * width), jnp.bfloat16),
            jax.ShapeDtypeStruct((rows, 2 * width), jnp.float32),
        ],
        compiler_params=pltpu.CompilerParams(vmem_limit_bytes=16 * MIB),
        cost_estimate=pl.CostEstimate(
            flops=4 * rows * page * width,
            bytes_accessed=rows * 2 * width * 6,
            transcendentals=rows * page,
        ),
        name="prepare_queries",
    )(q, cosine, sine, fresh_keys, fresh_values)


def attend_kernel(heads, factor, landing, live_ref, queries_ref, state_ref, all_ref, keys_ref,
                  values_ref, *refs):
    if landing:
        landed_ref, out_ref, placed_ref, rq_ref, acc_ref, top_ref, sem = refs
    else:
        out_ref, rq_ref, acc_ref, top_ref, sem = refs
    take_queries = pltpu.make_async_copy(queries_ref, rq_ref, sem.at[0])
    take_queries.start()
    take_state = pltpu.make_async_copy(state_ref, acc_ref, sem.at[1])
    take_state.start()
    if landing:
        place = pltpu.make_async_copy(landed_ref, placed_ref, sem.at[2])
        place.start()
    tokens, wide = out_ref.shape
    width = wide // heads
    page = all_ref.shape[4]
    pages = all_ref.shape[0]
    row = lax.broadcasted_iota(jnp.int32, (width, page), 0)

    def flags(p):
        hidden = jnp.where(live_ref[p] > 0, 0.0, -1e30)
        return jnp.where(row == 0, 1.0, jnp.where(row == 1, hidden, 0.0)).astype(jnp.bfloat16)

    def part_of(p, which):
        return jnp.concatenate([all_ref[p, 0, which], all_ref[p, 1, which]], axis=0)

    ones = jnp.ones((width, GROUPED * page), jnp.bfloat16)
    take_queries.wait()
    rq = rq_ref[...]
    for at in range(0, pages, GROUPED):
        weights = []
        for i in range(0, GROUPED, 2):
            keys = jnp.concatenate(
                [
                    jnp.concatenate([part_of(at + i + j, 0), flags(at + i + j)], axis=0)
                    for j in range(2)
                ],
                axis=1,
            )
            s = jnp.dot(rq, keys, preferred_element_type=jnp.float32)
            weights.append(jnp.exp2(s * factor).astype(jnp.bfloat16))
        values = jnp.concatenate([part_of(at + i, 1) for i in range(GROUPED)], axis=1)
        if at == 0:
            take_state.wait()
        acc_ref[...] += lax.dot_general(
            jnp.concatenate(weights, axis=1), jnp.concatenate([values, ones], axis=0),
            CONTRACT_LAST, preferred_element_type=jnp.float32,
        )

    @pl.when(jnp.logical_not(jnp.max(acc_ref[:, width:]) <= 1e30))
    def _():
        exact(factor, tokens, width, live_ref, rq_ref, keys_ref, values_ref,
              all_ref, acc_ref, top_ref)

    done = (acc_ref[:, :width] / acc_ref[:, width:]).astype(jnp.bfloat16)
    for h in range(heads):
        out_ref[:, h * width:(h + 1) * width] = done[h * tokens:(h + 1) * tokens, :]
    if landing:
        place.wait()


def exact(factor, tokens, width, live_ref, rq_ref, keys_ref, values_ref, all_ref, acc_ref, top_ref):
    rows = rq_ref.shape[0]
    pages = all_ref.shape[0]
    rq = rq_ref[:, :width]
    own = own_scores(rq, keys_ref[...], tokens)
    top_ref[...] = own

    def part_of(p, which):
        return jnp.concatenate([all_ref[p, 0, which], all_ref[p, 1, which]], axis=0)

    def scores_of(p):
        hidden = jnp.where(live_ref[p] > 0, 0.0, -1e30)
        return jnp.dot(rq, part_of(p, 0), preferred_element_type=jnp.float32) + hidden

    @pl.loop(0, pages)
    def _(p):
        top_ref[...] = jnp.maximum(top_ref[...], scores_of(p))

    top_ref[...] = jnp.broadcast_to(
        jnp.max(top_ref[...], axis=1, keepdims=True), top_ref.shape
    )
    w = jnp.exp2((own - top_ref[...]) * factor)
    acc_ref[:, :width] = lax.dot_general(
        w.astype(jnp.bfloat16), values_ref[...], CONTRACT_LAST,
        preferred_element_type=jnp.float32,
    )
    acc_ref[:, width:] = jnp.broadcast_to(jnp.sum(w, axis=1, keepdims=True), (rows, width))

    @pl.loop(0, pages)
    def _(p):
        w = jnp.exp2((scores_of(p) - top_ref[...]) * factor)
        acc_ref[:, :width] += lax.dot_general(
            w.astype(jnp.bfloat16), part_of(p, 1), CONTRACT_LAST, preferred_element_type=jnp.float32
        )
        acc_ref[:, width:] += jnp.broadcast_to(
            jnp.sum(w, axis=1, keepdims=True), (rows, width)
        )


def attend(tokens, live, rq, state, arrived, fresh_keys, fresh_values, landed=None):
    rows, double = rq.shape
    pages, _, _, half, page = arrived.shape
    width = double // 2
    heads = rows // tokens
    shape = (tokens, heads * width)
    landing = landed is not None
    vmem = pl.BlockSpec(memory_space=pltpu.VMEM)
    hbm = pl.BlockSpec(memory_space=pltpu.HBM)
    scratch = [
        pltpu.VMEM((rows, double), jnp.bfloat16),
        pltpu.VMEM((rows, double), jnp.float32),
        pltpu.VMEM((rows, page), jnp.float32),
        pltpu.SemaphoreType.DMA((3,)),
    ]
    more, more_specs = [], []
    out_shape, out_specs = [jax.ShapeDtypeStruct(shape, jnp.bfloat16)], [vmem]
    if landing:
        more, more_specs = [landed], [vmem]
        out_shape.append(jax.ShapeDtypeStruct(landed.shape, landed.dtype))
        out_specs.append(hbm)
    return pl.pallas_call(
        functools.partial(attend_kernel, heads, factor_of(width), landing),
        in_specs=[pl.BlockSpec(memory_space=pltpu.SMEM)] + [hbm] * 2 + [vmem] * 3 + more_specs,
        out_specs=out_specs,
        scratch_shapes=scratch,
        out_shape=out_shape,
        compiler_params=pltpu.CompilerParams(vmem_limit_bytes=24 * MIB),
        cost_estimate=pl.CostEstimate(
            flops=4 * rows * pages * page * width,
            bytes_accessed=pages * width * page * 4,
            transcendentals=rows * pages * page,
        ),
        name="attend_kept" if landing else "attend_sent",
    )(live, in_hbm(rq), in_hbm(state), arrived, fresh_keys, fresh_values, *more)


def on_device(pool_kv, queries, new_kv, page_table, prefix_pages):
    pool_count = lax.axis_size("pool")
    pool_rank = lax.axis_index("pool")
    core = lax.axis_index("core")
    lower_half = core == 0
    slot_count, _, half_width, page_len = pool_kv.shape
    head_width = 2 * half_width
    local_requests, suffix_len, _ = queries.shape
    owner_of = page_table // slot_count
    arrived = lax.all_to_all(
        pack(page_table, pool_kv), GROUP, split_axis=0, concat_axis=0, tiled=True
    ).reshape(pool_count, 2, 2, half_width, page_len)

    first_row = pool_rank * local_requests
    own_owners = lax.dynamic_index_in_dim(owner_of, first_row + core, 0, keepdims=False)
    owner_ids = jnp.arange(pool_count, dtype=jnp.int32)
    live = jnp.any(own_owners[None, :] == owner_ids[:, None], axis=1).astype(jnp.int32)
    own_lengths = lax.dynamic_slice_in_dim(prefix_pages, first_row, local_requests, 0)

    given = lax.dynamic_index_in_dim(queries, 1 - core, 0, keepdims=False)
    kept = lax.dynamic_index_in_dim(queries, core, 0, keepdims=False)
    other_fresh = swap_cores(new_kv)
    taken = swap_cores(given)

    positions = own_lengths[:, None] * page_len + jnp.arange(suffix_len, dtype=jnp.int32)
    angles = angles_of(positions.reshape(-1), head_width).reshape(
        local_requests, suffix_len, half_width
    )
    cosine, sine = jnp.cos(angles), jnp.sin(angles)
    own_cosine = lax.dynamic_index_in_dim(cosine, core, 0, keepdims=False)
    own_sine = lax.dynamic_index_in_dim(sine, core, 0, keepdims=False)
    q_cosine = jnp.concatenate([own_cosine, own_cosine], axis=1)
    q_sine = jnp.concatenate([-own_sine, own_sine], axis=1)

    first = jnp.where(lower_half, new_kv[:, 0], other_fresh[:, 0]).astype(jnp.float32)
    second = jnp.where(lower_half, other_fresh[:, 0], new_kv[:, 0]).astype(jnp.float32)
    k_cosine = jnp.swapaxes(cosine, 1, 2)
    k_sine = jnp.swapaxes(sine, 1, 2)
    rotated_first = (first * k_cosine - second * k_sine).astype(jnp.bfloat16)
    rotated_second = (second * k_cosine + first * k_sine).astype(jnp.bfloat16)
    own_keys = jnp.where(lower_half, rotated_first, rotated_second)
    landing = jnp.stack([own_keys, new_kv[:, 1]], axis=1)
    landed = from_behind(landing, "pool", pool_count // 2)

    fresh_keys = lax.dynamic_index_in_dim(
        jnp.concatenate([rotated_first, rotated_second], axis=1), core, 0, keepdims=False
    )
    mine = lax.dynamic_index_in_dim(new_kv[:, 1], core, 0, keepdims=False)
    theirs = lax.dynamic_index_in_dim(other_fresh[:, 1], core, 0, keepdims=False)
    fresh_values = jnp.where(
        lower_half,
        jnp.concatenate([mine, theirs], axis=0),
        jnp.concatenate([theirs, mine], axis=0),
    )

    sent = prepare(taken, q_cosine, q_sine, fresh_keys, fresh_values)
    kept = prepare(kept, q_cosine, q_sine, fresh_keys, fresh_values)
    arrived, sent, kept = lax.optimization_barrier((arrived, sent, kept))
    inputs = (arrived, fresh_keys, fresh_values)
    (for_partner,) = attend(suffix_len, live, *sent, *inputs)
    from_partner = swap_cores(for_partner)
    stays, landed = attend(suffix_len, live, *kept, *inputs, landed)
    attended = jnp.where(
        lower_half,
        jnp.stack([stays, from_partner], axis=0),
        jnp.stack([from_partner, stays], axis=0),
    )
    return (attended, landed)


def solution(mesh):
    pool_count, tp_count = mesh.devices.shape
    cores = Mesh(mesh.devices.reshape(pool_count, tp_count // 2, 2), ("pool", "head", "core"))
    tp = ("head", "core")
    return jax.shard_map(
        on_device,
        mesh=cores,
        in_specs=(
            P("pool", None, tp, None),
            P("pool", None, tp),
            P("pool", None, tp, None),
            P(),
            P(),
        ),
        out_specs=(P("pool", None, tp), P("pool", None, tp, None)),
        check_vma=False,
    )
```

```python
import functools
import math

import jax
import jax.numpy as jnp
from jax import lax
from jax.experimental import pallas as pl
from jax.experimental.pallas import tpu as pltpu
from jax.sharding import Mesh
from jax.sharding import PartitionSpec as P

MIB = 1024 * 1024
GROUP = ("pool", "core")
CONTRACT_LAST = (((1,), (1,)), ((), ()))
GROUPED = 8
UNROLL = 4


def factor_of(width):
    return math.log2(math.e) / math.sqrt(width)


def swap_cores(array):
    return lax.ppermute(array, "core", [(0, 1), (1, 0)])


def from_behind(array, axis, by):
    devices = lax.axis_size(axis)
    return lax.ppermute(array, axis, [(i, (i + by) % devices) for i in range(devices)])


def angles_of(positions, head_width):
    indices = jnp.arange(head_width // 2, dtype=jnp.float32)
    inverse = jnp.power(jnp.float32(1000000.0), -2.0 * indices / head_width)
    return positions.astype(jnp.float32)[:, None] * inverse[None, :]


def pack_kernel(table_ref, pool_ref, out_ref, held_ref, rows_ref, slots_ref, scalars_ref, sem):
    count = out_ref.shape[0]
    slot_count = pool_ref.shape[0]
    table = pltpu.make_async_copy(table_ref, rows_ref, sem.at[0])
    table.start()
    part = slot_count // 8
    for i in range(8):
        span = pl.ds(i * part, part)
        pltpu.make_async_copy(pool_ref.at[span], held_ref.at[span], sem.at[1]).start()
    table.wait()
    slot = rows_ref[...] - lax.axis_index("pool") * slot_count
    mine = jnp.logical_and(slot >= 0, slot < slot_count)
    slots_ref[...] = jnp.sum(jnp.where(mine, slot, 0), axis=0, keepdims=True)
    copy = pltpu.make_async_copy(slots_ref, scalars_ref, sem.at[2])
    copy.start()
    copy.wait()
    pltpu.make_async_copy(pool_ref, held_ref, sem.at[1]).wait()

    @pl.loop(0, count, unroll=16)
    def _(r):
        pltpu.make_async_copy(
            held_ref.at[scalars_ref[0, r]], out_ref.at[r], sem.at[3]
        ).start()

    pltpu.make_async_copy(out_ref, out_ref, sem.at[3]).wait()


def pack(page_table, pool_kv):
    requests, most = page_table.shape
    shape = (requests,) + pool_kv.shape[1:]
    hbm = pl.BlockSpec(memory_space=pltpu.HBM)
    return pl.pallas_call(
        pack_kernel,
        in_specs=[hbm, hbm],
        out_specs=hbm,
        scratch_shapes=[
            pltpu.VMEM(pool_kv.shape, pool_kv.dtype),
            pltpu.VMEM((most, requests), jnp.int32),
            pltpu.VMEM((1, requests), jnp.int32),
            pltpu.SMEM((1, requests), jnp.int32),
            pltpu.SemaphoreType.DMA((4,)),
        ],
        out_shape=jax.ShapeDtypeStruct(shape, pool_kv.dtype),
        compiler_params=pltpu.CompilerParams(vmem_limit_bytes=8 * MIB),
        cost_estimate=pl.CostEstimate(
            flops=0, bytes_accessed=4 * math.prod(shape), transcendentals=0
        ),
        name="pack_pages",
    )(
        pltpu.with_memory_space_constraint(page_table.T, pltpu.HBM),
        pltpu.with_memory_space_constraint(pool_kv, pltpu.HBM),
    )


def own_scores(rq, fresh_keys, tokens):
    rows, page = rq.shape[0], fresh_keys.shape[1]
    own = jnp.dot(rq, fresh_keys, preferred_element_type=jnp.float32)
    token = lax.rem(lax.broadcasted_iota(jnp.int32, (rows, page), 0), tokens)
    key = lax.broadcasted_iota(jnp.int32, (rows, page), 1)
    return jnp.where(key <= token, own, -1e30)


def prepare_kernel(heads, q_ref, cos_ref, sin_ref, keys_ref, rq_ref):
    tokens = q_ref.shape[0]
    width = cos_ref.shape[1]
    rows = heads * tokens
    parts = []
    for h in range(heads):
        x = q_ref[:, h * width:(h + 1) * width].astype(jnp.float32)
        turned = pltpu.roll(x, width // 2, 1)
        parts.append((x * cos_ref[...] + turned * sin_ref[...]).astype(jnp.bfloat16))
    rq = jnp.concatenate(parts, axis=0)
    own = own_scores(rq, keys_ref[...], tokens)
    shift = jnp.max(own, axis=1, keepdims=True).astype(jnp.bfloat16).astype(jnp.float32)
    lane = lax.broadcasted_iota(jnp.int32, (rows, width), 1)
    extra = jnp.where(lane == 0, -shift, jnp.where(lane == 1, 1.0, 0.0))
    rq_ref[:, :width] = rq
    rq_ref[:, width:] = extra.astype(jnp.bfloat16)


def prepare(q, cosine, sine, fresh_keys):
    tokens, wide = q.shape
    width, page = fresh_keys.shape
    heads = wide // width
    rows = heads * tokens
    vmem = pl.BlockSpec(memory_space=pltpu.VMEM)
    return pl.pallas_call(
        functools.partial(prepare_kernel, heads),
        in_specs=[vmem] * 4,
        out_specs=vmem,
        out_shape=jax.ShapeDtypeStruct((rows, 2 * width), jnp.bfloat16),
        compiler_params=pltpu.CompilerParams(vmem_limit_bytes=16 * MIB),
        cost_estimate=pl.CostEstimate(
            flops=2 * rows * page * width,
            bytes_accessed=rows * 2 * width * 2,
            transcendentals=0,
        ),
        name="prepare_queries",
    )(q, cosine, sine, fresh_keys)


def attend_kernel(heads, factor, landing, live_ref, rq_ref, all_ref, keys_ref,
                  values_ref, *refs):
    if landing:
        landed_ref, out_ref, placed_ref, acc_ref, top_ref, sem = refs
        place = pltpu.make_async_copy(landed_ref, placed_ref, sem)
        place.start()
    else:
        out_ref, acc_ref, top_ref = refs
    tokens, wide = out_ref.shape
    width = wide // heads
    page = all_ref.shape[4]
    pages = all_ref.shape[0]
    row = lax.broadcasted_iota(jnp.int32, (width, page), 0)

    def flags(p):
        hidden = jnp.where(live_ref[p] > 0, 0.0, -1e30)
        return jnp.where(row == 0, 1.0, jnp.where(row == 1, hidden, 0.0)).astype(jnp.bfloat16)

    def part_of(p, which):
        return jnp.concatenate([all_ref[p, 0, which], all_ref[p, 1, which]], axis=0)

    ones = jnp.ones((width, GROUPED * page), jnp.bfloat16)
    rq = rq_ref[...]
    rows = rq.shape[0]
    token = lax.rem(lax.broadcasted_iota(jnp.int32, (rows, page), 0), tokens)
    key = lax.broadcasted_iota(jnp.int32, (rows, page), 1)
    new_keys = jnp.concatenate(
        [keys_ref[...], jnp.where(row == 0, 1.0, 0.0).astype(jnp.bfloat16)], axis=0
    )
    s = jnp.dot(rq, new_keys, preferred_element_type=jnp.float32)
    w = jnp.exp2(jnp.where(key <= token, s, -1e30) * factor)
    acc_ref[...] = lax.dot_general(
        w.astype(jnp.bfloat16),
        jnp.concatenate([values_ref[...], ones[:, :page]], axis=0),
        CONTRACT_LAST, preferred_element_type=jnp.float32,
    )

    @pl.loop(0, pages // GROUPED, unroll=UNROLL)
    def _(g):
        at = g * GROUPED
        weights = []
        for i in range(0, GROUPED, 2):
            keys = jnp.concatenate(
                [
                    jnp.concatenate([part_of(at + i + j, 0), flags(at + i + j)], axis=0)
                    for j in range(2)
                ],
                axis=1,
            )
            s = jnp.dot(rq, keys, preferred_element_type=jnp.float32)
            weights.append(jnp.exp2(s * factor).astype(jnp.bfloat16))
        values = jnp.concatenate([part_of(at + i, 1) for i in range(GROUPED)], axis=1)
        acc_ref[...] += lax.dot_general(
            jnp.concatenate(weights, axis=1), jnp.concatenate([values, ones], axis=0),
            CONTRACT_LAST, preferred_element_type=jnp.float32,
        )

    @pl.when(jnp.logical_not(jnp.max(acc_ref[:, width:]) <= 1e30))
    def _():
        exact(factor, tokens, width, live_ref, rq_ref, keys_ref, values_ref,
              all_ref, acc_ref, top_ref)

    done = (acc_ref[:, :width] / acc_ref[:, width:]).astype(jnp.bfloat16)
    for h in range(heads):
        out_ref[:, h * width:(h + 1) * width] = done[h * tokens:(h + 1) * tokens, :]
    if landing:
        place.wait()


def exact(factor, tokens, width, live_ref, rq_ref, keys_ref, values_ref, all_ref, acc_ref, top_ref):
    rows = rq_ref.shape[0]
    pages = all_ref.shape[0]
    rq = rq_ref[:, :width]
    own = own_scores(rq, keys_ref[...], tokens)
    top_ref[...] = own

    def part_of(p, which):
        return jnp.concatenate([all_ref[p, 0, which], all_ref[p, 1, which]], axis=0)

    def scores_of(p):
        hidden = jnp.where(live_ref[p] > 0, 0.0, -1e30)
        return jnp.dot(rq, part_of(p, 0), preferred_element_type=jnp.float32) + hidden

    @pl.loop(0, pages)
    def _(p):
        top_ref[...] = jnp.maximum(top_ref[...], scores_of(p))

    top_ref[...] = jnp.broadcast_to(
        jnp.max(top_ref[...], axis=1, keepdims=True), top_ref.shape
    )
    w = jnp.exp2((own - top_ref[...]) * factor)
    acc_ref[:, :width] = lax.dot_general(
        w.astype(jnp.bfloat16), values_ref[...], CONTRACT_LAST,
        preferred_element_type=jnp.float32,
    )
    acc_ref[:, width:] = jnp.broadcast_to(jnp.sum(w, axis=1, keepdims=True), (rows, width))

    @pl.loop(0, pages)
    def _(p):
        w = jnp.exp2((scores_of(p) - top_ref[...]) * factor)
        acc_ref[:, :width] += lax.dot_general(
            w.astype(jnp.bfloat16), part_of(p, 1), CONTRACT_LAST, preferred_element_type=jnp.float32
        )
        acc_ref[:, width:] += jnp.broadcast_to(
            jnp.sum(w, axis=1, keepdims=True), (rows, width)
        )


def attend(tokens, live, rq, arrived, fresh_keys, fresh_values, landed=None):
    rows, double = rq.shape
    pages, _, _, half, page = arrived.shape
    width = double // 2
    heads = rows // tokens
    shape = (tokens, heads * width)
    landing = landed is not None
    vmem = pl.BlockSpec(memory_space=pltpu.VMEM)
    scratch = [pltpu.VMEM((rows, double), jnp.float32), pltpu.VMEM((rows, page), jnp.float32)]
    more, more_specs = [], []
    out_shape, out_specs = [jax.ShapeDtypeStruct(shape, jnp.bfloat16)], [vmem]
    if landing:
        more, more_specs = [landed], [vmem]
        out_shape.append(jax.ShapeDtypeStruct(landed.shape, landed.dtype))
        out_specs.append(pl.BlockSpec(memory_space=pltpu.HBM))
        scratch.append(pltpu.SemaphoreType.DMA)
    return pl.pallas_call(
        functools.partial(attend_kernel, heads, factor_of(width), landing),
        in_specs=[pl.BlockSpec(memory_space=pltpu.SMEM)] + [vmem] * 4 + more_specs,
        out_specs=out_specs,
        scratch_shapes=scratch,
        out_shape=out_shape,
        compiler_params=pltpu.CompilerParams(vmem_limit_bytes=24 * MIB),
        cost_estimate=pl.CostEstimate(
            flops=4 * rows * pages * page * width,
            bytes_accessed=pages * width * page * 4,
            transcendentals=rows * pages * page,
        ),
        name="attend_kept" if landing else "attend_sent",
    )(live, rq, arrived, fresh_keys, fresh_values, *more)


def on_device(pool_kv, queries, new_kv, page_table, prefix_pages):
    pool_count = lax.axis_size("pool")
    pool_rank = lax.axis_index("pool")
    core = lax.axis_index("core")
    lower_half = core == 0
    slot_count, _, half_width, page_len = pool_kv.shape
    head_width = 2 * half_width
    local_requests, suffix_len, _ = queries.shape
    owner_of = page_table // slot_count
    arrived = lax.all_to_all(
        pack(page_table, pool_kv), GROUP, split_axis=0, concat_axis=0, tiled=True
    ).reshape(pool_count, 2, 2, half_width, page_len)

    first_row = pool_rank * local_requests
    own_owners = lax.dynamic_index_in_dim(owner_of, first_row + core, 0, keepdims=False)
    owner_ids = jnp.arange(pool_count, dtype=jnp.int32)
    live = jnp.any(own_owners[None, :] == owner_ids[:, None], axis=1).astype(jnp.int32)
    own_lengths = lax.dynamic_slice_in_dim(prefix_pages, first_row, local_requests, 0)

    given = lax.dynamic_index_in_dim(queries, 1 - core, 0, keepdims=False)
    kept = lax.dynamic_index_in_dim(queries, core, 0, keepdims=False)
    other_fresh = swap_cores(new_kv)
    taken = swap_cores(given)

    positions = own_lengths[:, None] * page_len + jnp.arange(suffix_len, dtype=jnp.int32)
    angles = angles_of(positions.reshape(-1), head_width).reshape(
        local_requests, suffix_len, half_width
    )
    cosine, sine = jnp.cos(angles), jnp.sin(angles)
    own_cosine = lax.dynamic_index_in_dim(cosine, core, 0, keepdims=False)
    own_sine = lax.dynamic_index_in_dim(sine, core, 0, keepdims=False)
    q_cosine = jnp.concatenate([own_cosine, own_cosine], axis=1)
    q_sine = jnp.concatenate([-own_sine, own_sine], axis=1)

    first = jnp.where(lower_half, new_kv[:, 0], other_fresh[:, 0]).astype(jnp.float32)
    second = jnp.where(lower_half, other_fresh[:, 0], new_kv[:, 0]).astype(jnp.float32)
    k_cosine = jnp.swapaxes(cosine, 1, 2)
    k_sine = jnp.swapaxes(sine, 1, 2)
    rotated_first = (first * k_cosine - second * k_sine).astype(jnp.bfloat16)
    rotated_second = (second * k_cosine + first * k_sine).astype(jnp.bfloat16)
    own_keys = jnp.where(lower_half, rotated_first, rotated_second)
    landing = jnp.stack([own_keys, new_kv[:, 1]], axis=1)
    landed = from_behind(landing, "pool", pool_count // 2)

    fresh_keys = lax.dynamic_index_in_dim(
        jnp.concatenate([rotated_first, rotated_second], axis=1), core, 0, keepdims=False
    )
    mine = lax.dynamic_index_in_dim(new_kv[:, 1], core, 0, keepdims=False)
    theirs = lax.dynamic_index_in_dim(other_fresh[:, 1], core, 0, keepdims=False)
    fresh_values = jnp.where(
        lower_half,
        jnp.concatenate([mine, theirs], axis=0),
        jnp.concatenate([theirs, mine], axis=0),
    )

    sent = prepare(taken, q_cosine, q_sine, fresh_keys)
    kept = prepare(kept, q_cosine, q_sine, fresh_keys)
    arrived, sent, kept = lax.optimization_barrier((arrived, sent, kept))
    inputs = (arrived, fresh_keys, fresh_values)
    (for_partner,) = attend(suffix_len, live, sent, *inputs)
    from_partner = swap_cores(for_partner)
    stays, landed = attend(suffix_len, live, kept, *inputs, landed)
    attended = jnp.where(
        lower_half,
        jnp.stack([stays, from_partner], axis=0),
        jnp.stack([from_partner, stays], axis=0),
    )
    return (attended, landed)


def solution(mesh):
    pool_count, tp_count = mesh.devices.shape
    cores = Mesh(mesh.devices.reshape(pool_count, tp_count // 2, 2), ("pool", "head", "core"))
    tp = ("head", "core")
    return jax.shard_map(
        on_device,
        mesh=cores,
        in_specs=(
            P("pool", None, tp, None),
            P("pool", None, tp),
            P("pool", None, tp, None),
            P(),
            P(),
        ),
        out_specs=(P("pool", None, tp), P("pool", None, tp, None)),
        check_vma=False,
    )
```
